32 devices in a mesh: group: 4 (over z), member: 8 (over y, x, core).
Axes of the slice: x: 2, y: 2, z: 4, core: 2. Of those that a mesh axis runs over, the one named last changes fastest.
Arguments:
- embeddings: bfloat16 [16384, 768], P(('group', 'member')), may hold values from -120 to 120
- cluster_ids: int32 [16384], P(('group', 'member')), may hold values from 0 to 63, as said below
- ranks: int32 [16384], P(('group', 'member')), may hold values from 0 to 16383, each once
Outputs:
- best_similarity: float32 [16384], P(('group', 'member'))
The draws below stay inside these ranges and needn't reach their ends.
Inputs may be any that keep to these rules, and one draw needn't show every extreme that they name: `cluster_ids`: among the 512 rows of any one device, one residue of the cluster ids modulo 4 has exactly 256 rows, the next residue (modulo 4) none, and every other residue 512 // 4; which residue has 256 depends only on the device's member index, so every residue has exactly 4096 rows in all. The 16 clusters of one residue hold, in some order, (l+1)**2 * 4096 // 16**2 - l**2 * 4096 // 16**2 rows for l = 0 to 15; the largest holds 496.
All inputs are finite; a program needn't handle non-finite values.
Results may differ from the reference program's by a relative error of at most 0.00058.
Values may be sent and summed in bfloat16 or wider, within the bound.
A program may use at most 128 MiB of HBM per device.

```python
import math
import jax
import jax.numpy as jnp
from jax import lax

D = 768
ROW_DEV = 512
CLUSTERS = 64
DUPS = 8
GROUPS = 4
MEMBERS = 8
ROWS = 16384


def cluster_plan(key):
    blocks = ROWS // ROW_DEV
    share = ROW_DEV // GROUPS
    capacity = 2 * share
    per_group = CLUSTERS // GROUPS
    group_rows = ROWS // GROUPS
    key_rot, key_perm, key_pos, key_local = jax.random.split(key, 4)
    rotation = jax.random.randint(key_rot, (), 0, GROUPS)
    block_ids = jnp.arange(blocks, dtype=jnp.int32)
    heavy = (block_ids % MEMBERS + rotation) % GROUPS
    places = jax.vmap(lambda sub: jax.random.permutation(sub, ROW_DEV))(jax.random.split(key_perm, blocks))
    offset = jnp.where(places < capacity, 0, 2 + (places - capacity) // share)
    residue = ((heavy[:, None] + offset) % GROUPS).reshape(ROWS).astype(jnp.int32)
    lanes = jnp.arange(GROUPS, dtype=jnp.int32)
    hits = (residue[:, None] == lanes[None, :]).astype(jnp.int32)
    order = jnp.sum((jnp.cumsum(hits, axis=0) - hits) * hits, axis=1).astype(jnp.int32)
    shuffles = jax.vmap(lambda sub: jax.random.permutation(sub, group_rows))(jax.random.split(key_pos, GROUPS))
    shuffled = shuffles[residue, order]
    levels = jnp.arange(1, per_group, dtype=jnp.int32)
    bounds = levels * levels * group_rows // (per_group * per_group)
    slot_of = jnp.sum((bounds[None, :] <= shuffled[:, None]).astype(jnp.int32), axis=1)
    local_perm = jax.vmap(lambda sub: jax.random.permutation(sub, per_group))(jax.random.split(key_local, GROUPS))
    cluster = residue + GROUPS * local_perm[residue, slot_of]
    return cluster.astype(jnp.int32)


def draw_cluster_ids(key, part):
    return cluster_plan(key)


def draw_embeddings(key, part):
    cluster = cluster_plan(key)
    key = jax.random.fold_in(key, 11)
    key_cen, key_fam, key_twin, key_mix, key_own, key_spread, key_col, key_row = jax.random.split(key, 8)
    centers = jax.random.truncated_normal(key_cen, -4.0, 4.0, (CLUSTERS, D), jnp.float32)
    family = jax.random.truncated_normal(key_fam, -4.0, 4.0, (CLUSTERS * DUPS, D), jnp.float32)
    twin = jax.random.randint(key_twin, (ROWS,), 0, DUPS)
    mixing = jax.random.uniform(key_mix, (ROWS, 1), jnp.float32, 0.0, 0.95)
    spread = jnp.exp(jax.random.uniform(key_spread, (ROWS, 1), jnp.float32, math.log(0.3), 0.0))
    own = jax.random.truncated_normal(key_own, -4.0, 4.0, (ROWS, D), jnp.float32)
    column = jnp.exp(jax.random.uniform(key_col, (D,), jnp.float32, math.log(0.4), math.log(2.5)))
    row_scale = jnp.exp(jax.random.uniform(key_row, (ROWS, 1), jnp.float32, math.log(0.5), math.log(2.0)))
    noise = jnp.sqrt(1.0 - mixing * mixing) * own + mixing * family[cluster * DUPS + twin]
    base = 0.5 * centers[cluster] + spread * noise
    return (base * column[None, :] * row_scale).astype(jnp.bfloat16)


def setup_inputs(seed: int = 0) -> dict:
    streams_of = jax.random.split(jax.random.key(seed), 4)
    embeddings = draw_embeddings(jax.random.fold_in(streams_of[3], 71), 0)
    cluster_ids = draw_cluster_ids(jax.random.fold_in(streams_of[3], 71), 0)
    ranks = jax.random.permutation(streams_of[2], ROWS).astype(jnp.int32)
    return dict(embeddings=embeddings, cluster_ids=cluster_ids, ranks=ranks)


def unit_rows(values):
    widened = values.astype(jnp.float32)
    square = lax.optimization_barrier(jnp.mean(widened * widened, axis=-1, keepdims=True))
    return (widened * lax.rsqrt(square + 1e-06) * (1.0 / math.sqrt(values.shape[-1]))).astype(jnp.bfloat16)

def reference(embeddings, cluster_ids, ranks):
    key_units = unit_rows(embeddings).astype(jnp.float32)
    block_rows = math.gcd(ROWS, 512)
    block_count = ROWS // block_rows

    def one_block(position):
        offset = position * block_rows
        query_units = lax.dynamic_slice_in_dim(key_units, offset, block_rows, 0)
        query_ids = lax.dynamic_slice_in_dim(cluster_ids, offset, block_rows, 0)
        query_ranks = lax.dynamic_slice_in_dim(ranks, offset, block_rows, 0)
        scores = jnp.dot(query_units, key_units.T, preferred_element_type=jnp.float32)
        allowed = (query_ids[:, None] == cluster_ids[None, :]) & (ranks[None, :] < query_ranks[:, None])
        return lax.optimization_barrier(jnp.max(jnp.where(allowed, scores, -1.0), axis=1))
    return lax.map(one_block, jnp.arange(block_count, dtype=jnp.int32)).reshape(ROWS)
```

```python
import functools
import math

import jax
import jax.numpy as jnp
from jax import lax
from jax.experimental import pallas as pl
from jax.experimental.pallas import tpu as pltpu
from jax.sharding import PartitionSpec as P

META = 128


def flip(index, mask):
    result = index
    bit = 1
    while bit <= mask:
        if mask & bit:
            result = result + bit - 2 * bit * lax.rem(lax.div(index, bit), 2)
        bit *= 2
    return result


def kernel(
    groups,
    members,
    emb_ref,
    ids_ref,
    ranks_ref,
    out_ref,
    packed,
    send1,
    recv1,
    send2,
    held,
    score2,
    back2,
    score1,
    back1,
    s1_send,
    s1_recv,
    s2_send,
    s2_recv,
    ag_send,
    ag_recv,
    b2_send,
    b2_recv,
    b1_send,
    b1_recv,
):
    rows, features = emb_ref.shape
    width = features + META
    deal = rows // members
    share = rows // groups
    z = lax.axis_index("group")
    m = lax.axis_index("member")

    barrier = pltpu.get_barrier_semaphore()
    for r in range(1, members):
        pl.semaphore_signal(
            barrier, inc=1, device_id=(z, flip(m, r)), device_id_type=pl.DeviceIdType.MESH
        )
    for d in range(1, groups):
        pl.semaphore_signal(
            barrier, inc=1, device_id=(flip(z, d), m), device_id_type=pl.DeviceIdType.MESH
        )

    def push(src, dst, send_sem, recv_sem, where):
        copy = pltpu.make_async_remote_copy(
            src_ref=src,
            dst_ref=dst,
            send_sem=send_sem,
            recv_sem=recv_sem,
            device_id=where,
            device_id_type=pl.DeviceIdType.MESH,
        )
        copy.start()
        return copy

    def column(row):
        return jnp.broadcast_to(row, (8, rows)).T[:, 0:1]

    sub = lax.broadcasted_iota(jnp.int32, (rows, rows), 0)
    lane = lax.broadcasted_iota(jnp.int32, (1, rows), 1)

    def order(bucket_row):
        key_row = (bucket_row * rows + lane).astype(jnp.float32)
        key_col = column(key_row)
        return jnp.sum((key_col < key_row).astype(jnp.float32), axis=0, keepdims=True).astype(
            jnp.int32
        )

    widened = emb_ref[...].astype(jnp.float32)
    square = jnp.mean(widened * widened, axis=-1, keepdims=True)
    packed[:, :features] = (
        widened * lax.rsqrt(square + 1e-06) * (1.0 / math.sqrt(features))
    ).astype(jnp.bfloat16)
    ids = ids_ref[...]
    ranks = ranks_ref[...]
    residue = lax.rem(ids, groups)
    level = lax.broadcasted_iota(jnp.int32, (META, rows), 0)
    high = lax.div(ranks, 256)
    fields = jnp.where(
        level == 0,
        ids,
        jnp.where(
            level == 1,
            high,
            jnp.where(level == 2, ranks - high * 256, jnp.where(level == 3, residue, 0)),
        ),
    )
    packed[:, features:] = fields.astype(jnp.float32).T.astype(jnp.bfloat16)

    place = order(residue)
    slot1 = jnp.bitwise_xor(lax.rem(place, members), m) * deal + lax.div(place, members)
    send1[...] = jnp.dot(
        (sub == slot1).astype(jnp.float32).astype(jnp.bfloat16),
        packed[...],
        preferred_element_type=jnp.float32,
    ).astype(jnp.bfloat16)
    pl.semaphore_wait(barrier, members + groups - 2)
    copies1 = [
        push(
            send1.at[pl.ds(r * deal, deal)],
            recv1.at[pl.ds(r * deal, deal)],
            s1_send.at[r],
            s1_recv.at[r],
            (z, flip(m, r)),
        )
        for r in range(members - 1, 0, -1)
    ]
    recv1[:deal] = send1[:deal]
    for copy in copies1:
        copy.wait_recv()

    residue2 = recv1[:, features:].astype(jnp.float32).T[3:4].astype(jnp.int32)
    slot2 = order(jnp.bitwise_xor(residue2, z))
    send2[...] = jnp.dot(
        (sub == slot2).astype(jnp.float32).astype(jnp.bfloat16),
        recv1[...],
        preferred_element_type=jnp.float32,
    ).astype(jnp.bfloat16)
    copies2 = {
        d: push(
            send2.at[pl.ds(d * share, share)],
            held.at[0, pl.ds(d * share, share)],
            s2_send.at[d],
            s2_recv.at[d],
            (flip(z, d), m),
        )
        for d in range(groups - 1, 0, -1)
    }
    held[0, :share] = send2[:share]

    gathers = {}
    half = share // 2

    def forward(source, slot, d, part, hop):
        start = d * share + (0 if part is None else part * half)
        span = pl.ds(start, share if part is None else half)
        index = (slot, d, part or 0)
        gathers[(slot, d, part)] = push(
            held.at[source, span],
            held.at[slot, span],
            ag_send.at[index],
            ag_recv.at[index],
            (z, flip(m, hop)),
        )

    def arrive(slot, d, part=None):
        gathers[(slot, d, part)].wait_recv()

    tree = members == 8 and groups == 4

    def own_chunk(d):
        if d:
            copies2[d].wait_recv()
        for r in (2, 4, 1) if tree else range(1, members):
            forward(0, r, d, None, r)

    def pass_on(d):
        arrive(2, d)
        forward(2, 6, d, 0, 4)
        forward(2, 3, d, None, 1)
        arrive(4, d)
        forward(4, 6, d, 1, 2)
        forward(4, 5, d, None, 1)

    def pass_diagonal(d):
        for part in (0, 1):
            arrive(6, d, part)
            forward(6, 7, d, part, 1)

    for d in range(groups):
        own_chunk(d)
        if tree and d >= 1:
            pass_on(d - 1)
        if tree and d >= 2:
            pass_diagonal(d - 2)

    query_fields = held[0, :, features:].astype(jnp.float32).T
    query_low = query_fields[0:1] * 65536.0
    query_key = query_low + query_fields[1:2] * 256.0 + query_fields[2:3]

    def scored(r, best):
        scores = lax.dot_general(
            held[r, :, :features],
            held[0, :, :features],
            (((1,), (1,)), ((), ())),
            preferred_element_type=jnp.float32,
        )
        fields = held[r, :, features:].astype(jnp.float32)
        key = fields[:, 0:1] * 65536.0 + fields[:, 1:2] * 256.0 + fields[:, 2:3]
        allowed = (key >= query_low) & (key < query_key)
        return jnp.maximum(
            best, jnp.max(jnp.where(allowed, scores, -1.0), axis=0, keepdims=True)
        )

    best = jnp.full((1, rows), -1.0, jnp.float32)
    if tree:
        pass_on(groups - 1)
        pass_diagonal(groups - 2)
        best = scored(0, best)
        for r in (2, 4):
            best = scored(r, best)
        pass_diagonal(groups - 1)
        for r in (1, 3, 5):
            for d in range(groups):
                arrive(r, d)
            best = scored(r, best)
        best = scored(6, best)
        for d in range(groups):
            for part in (0, 1):
                arrive(7, d, part)
        best = scored(7, best)
    else:
        best = scored(0, best)
        for r in range(1, members):
            for d in range(groups):
                arrive(r, d)
            best = scored(r, best)

    score2[...] = best
    home2 = [
        push(score2, back2.at[d], b2_send.at[d], b2_recv.at[d], (flip(z, d), m))
        for d in range(groups - 1, 0, -1)
    ]
    for copy in home2:
        copy.wait_recv()
    merged = best
    for d in range(1, groups):
        merged = jnp.where(lax.div(lane, share) == d, back2[d], merged)
    best = jnp.max(jnp.where(sub == slot2, column(merged), -2.0), axis=0, keepdims=True)
    score1[...] = best
    home1 = [
        push(score1, back1.at[r], b1_send.at[r], b1_recv.at[r], (z, flip(m, r)))
        for r in range(members - 1, 0, -1)
    ]
    for copy in home1:
        copy.wait_recv()
    merged = best
    for r in range(1, members):
        merged = jnp.where(lax.div(lane, deal) == r, back1[r], merged)
    out_ref[...] = jnp.max(jnp.where(sub == slot1, column(merged), -2.0), axis=0, keepdims=True)

    for copy in [*copies1, *copies2.values(), *gathers.values(), *home2, *home1]:
        copy.wait_send()


def body(embeddings, cluster_ids, ranks):
    rows, features = embeddings.shape
    groups = lax.axis_size("group")
    members = lax.axis_size("member")
    width = features + META
    scores = pl.pallas_call(
        functools.partial(kernel, groups, members),
        out_shape=jax.ShapeDtypeStruct((1, rows), jnp.float32),
        in_specs=[pl.BlockSpec(memory_space=pltpu.VMEM)] * 3,
        out_specs=pl.BlockSpec(memory_space=pltpu.VMEM),
        scratch_shapes=[
            pltpu.VMEM((rows, width), jnp.bfloat16),
            pltpu.VMEM((rows, width), jnp.bfloat16),
            pltpu.VMEM((rows, width), jnp.bfloat16),
            pltpu.VMEM((rows, width), jnp.bfloat16),
            pltpu.VMEM((members, rows, width), jnp.bfloat16),
            pltpu.VMEM((1, rows), jnp.float32),
            pltpu.VMEM((groups, 1, rows), jnp.float32),
            pltpu.VMEM((1, rows), jnp.float32),
            pltpu.VMEM((members, 1, rows), jnp.float32),
            pltpu.SemaphoreType.DMA((members,)),
            pltpu.SemaphoreType.DMA((members,)),
            pltpu.SemaphoreType.DMA((groups,)),
            pltpu.SemaphoreType.DMA((groups,)),
            pltpu.SemaphoreType.DMA((members, groups, 2)),
            pltpu.SemaphoreType.DMA((members, groups, 2)),
            pltpu.SemaphoreType.DMA((groups,)),
            pltpu.SemaphoreType.DMA((groups,)),
            pltpu.SemaphoreType.DMA((members,)),
            pltpu.SemaphoreType.DMA((members,)),
        ],
        compiler_params=pltpu.CompilerParams(
            collective_id=0, has_side_effects=True, vmem_limit_bytes=48 * 1024 * 1024
        ),
    )(embeddings, cluster_ids.reshape(1, rows), ranks.reshape(1, rows))
    return scores.reshape(rows)


def solution(mesh):
    return jax.shard_map(
        body,
        mesh=mesh,
        in_specs=(P(("group", "member"), None), P(("group", "member")), P(("group", "member"))),
        out_specs=P(("group", "member")),
        check_vma=False,
    )
```

```python
import functools
import math

import jax
import jax.numpy as jnp
from jax import lax
from jax.experimental import pallas as pl
from jax.experimental.pallas import tpu as pltpu
from jax.sharding import PartitionSpec as P


def flip(index, mask):
    result = index
    bit = 1
    while bit <= mask:
        if mask & bit:
            result = result + bit - 2 * bit * lax.rem(lax.div(index, bit), 2)
        bit *= 2
    return result


def kernel(
    groups,
    members,
    emb_ref,
    ids_ref,
    ranks_ref,
    out_ref,
    emb,
    ids_row,
    ranks_row,
    packed,
    send1,
    recv1,
    send2,
    held,
    key1,
    keyin1,
    key2,
    keyin2,
    keys,
    score2,
    back2,
    score1,
    back1,
    local,
    s1_send,
    s1_recv,
    s2_send,
    s2_recv,
    ag_send,
    ag_recv,
    k1_send,
    k1_recv,
    k2_send,
    k2_recv,
    k3_send,
    k3_recv,
    b2_send,
    b2_recv,
    b1_send,
    b1_recv,
):
    rows, features = emb_ref.shape
    deal = rows // members
    share = rows // groups
    z = lax.axis_index("group")
    m = lax.axis_index("member")

    loads = [
        pltpu.make_async_copy(src, dst, local.at[n])
        for n, (src, dst) in enumerate(
            ((ids_ref, ids_row), (ranks_ref, ranks_row), (emb_ref, emb))
        )
    ]
    for load in loads:
        load.start()
    barrier = pltpu.get_barrier_semaphore()
    for r in range(1, members):
        pl.semaphore_signal(
            barrier, inc=1, device_id=(z, flip(m, r)), device_id_type=pl.DeviceIdType.MESH
        )
    for d in range(1, groups):
        pl.semaphore_signal(
            barrier, inc=1, device_id=(flip(z, d), m), device_id_type=pl.DeviceIdType.MESH
        )

    def push(src, dst, send_sem, recv_sem, where):
        copy = pltpu.make_async_remote_copy(
            src_ref=src,
            dst_ref=dst,
            send_sem=send_sem,
            recv_sem=recv_sem,
            device_id=where,
            device_id_type=pl.DeviceIdType.MESH,
        )
        copy.start()
        return copy

    def column(row):
        return jnp.broadcast_to(row, (8, rows)).T[:, 0:1]

    sub = lax.broadcasted_iota(jnp.int32, (rows, rows), 0)
    lane = lax.broadcasted_iota(jnp.int32, (1, rows), 1)

    def order(bucket_row):
        key_row = (bucket_row * rows + lane).astype(jnp.float32)
        key_col = column(key_row)
        return jnp.sum((key_col < key_row).astype(jnp.float32), axis=0, keepdims=True).astype(
            jnp.int32
        )

    def permutation(slot):
        return (sub == slot).astype(jnp.float32).astype(jnp.bfloat16)

    def place_keys(ids, ranks, chosen):
        level = lax.broadcasted_iota(jnp.int32, (16, rows), 0)
        high = lax.div(ranks, 256)
        fields = jnp.where(
            level == 0, ids, jnp.where(level == 1, high, jnp.where(level == 2, ranks - high * 256, 0))
        )
        placed = lax.dot_general(
            fields.astype(jnp.float32).astype(jnp.bfloat16),
            chosen,
            (((1,), (1,)), ((), ())),
            preferred_element_type=jnp.float32,
        )
        return placed[0:1] * 65536.0 + placed[1:2] * 256.0 + placed[2:3]

    loads[0].wait()
    loads[1].wait()
    ids = ids_row[...]
    place = order(lax.rem(ids, groups))
    slot1 = jnp.bitwise_xor(lax.rem(place, members), m) * deal + lax.div(place, members)
    chosen1 = permutation(slot1)
    key1[...] = place_keys(ids, ranks_row[...], chosen1)
    loads[2].wait()
    widened = emb[...].astype(jnp.float32)
    square = jnp.mean(widened * widened, axis=-1, keepdims=True)
    packed[...] = (widened * lax.rsqrt(square + 1e-06) * (1.0 / math.sqrt(features))).astype(
        jnp.bfloat16
    )
    send1[...] = jnp.dot(chosen1, packed[...], preferred_element_type=jnp.float32).astype(
        jnp.bfloat16
    )
    pl.semaphore_wait(barrier, members + groups - 2)
    small = []
    for r in range(1, members):
        small.append(push(key1, keyin1.at[r], k1_send.at[r], k1_recv.at[r], (z, flip(m, r))))
    copies1 = [
        push(
            send1.at[pl.ds(r * deal, deal)],
            recv1.at[pl.ds(r * deal, deal)],
            s1_send.at[r],
            s1_recv.at[r],
            (z, flip(m, r)),
        )
        for r in range(members - 1, 0, -1)
    ]
    recv1[:deal] = send1[:deal]

    merged = key1[...]
    for r in range(1, members):
        small[r - 1].wait_recv()
        merged = jnp.where(lax.div(lane, deal) == r, keyin1[r], merged)
    merged = merged.astype(jnp.int32)
    ids = lax.div(merged, 65536)
    slot2 = order(jnp.bitwise_xor(lax.rem(ids, groups), z))
    chosen2 = permutation(slot2)
    key2[...] = place_keys(ids, merged - ids * 65536, chosen2)
    small2 = [
        push(key2, keyin2.at[d], k2_send.at[d], k2_recv.at[d], (flip(z, d), m))
        for d in range(1, groups)
    ]
    for copy in copies1:
        copy.wait_recv()
    send2[...] = jnp.dot(chosen2, recv1[...], preferred_element_type=jnp.float32).astype(
        jnp.bfloat16
    )
    copies2 = {
        d: push(
            send2.at[pl.ds(d * share, share)],
            held.at[0, pl.ds(d * share, share)],
            s2_send.at[d],
            s2_recv.at[d],
            (flip(z, d), m),
        )
        for d in range(1, groups)
    }
    held[0, :share] = send2[:share]

    gathers = {}
    half = share // 2

    def forward(source, slot, d, part, hop):
        start = d * share + (0 if part is None else part * half)
        span = pl.ds(start, share if part is None else half)
        index = (slot, d, part or 0)
        gathers[(slot, d, part)] = push(
            held.at[source, span],
            held.at[slot, span],
            ag_send.at[index],
            ag_recv.at[index],
            (z, flip(m, hop)),
        )

    def arrive(slot, d, part=None):
        gathers[(slot, d, part)].wait_recv()

    tree = members == 8 and groups == 4

    def own_chunk(d):
        if d:
            copies2[d].wait_recv()
        for r in (2, 4, 1) if tree else range(1, members):
            forward(0, r, d, None, r)

    def pass_on(d):
        arrive(2, d)
        forward(2, 6, d, 0, 4)
        forward(2, 3, d, None, 1)
        arrive(4, d)
        forward(4, 6, d, 1, 2)
        forward(4, 5, d, None, 1)

    def pass_diagonal(d):
        for part in (0, 1):
            arrive(6, d, part)
            forward(6, 7, d, part, 1)

    own_chunk(0)
    merged = key2[...]
    for d in range(1, groups):
        small2[d - 1].wait_recv()
        merged = jnp.where(lax.div(lane, share) == d, keyin2[d], merged)
    keys[0] = merged
    small3 = [
        push(keys.at[0], keys.at[r], k3_send.at[r], k3_recv.at[r], (z, flip(m, r)))
        for r in range(1, members)
    ]
    query_key = merged
    query_low = (lax.div(merged.astype(jnp.int32), 65536) * 65536).astype(jnp.float32)

    for d in range(1, groups):
        own_chunk(d)
        if tree:
            pass_on(d - 1)
        if tree and d >= 2:
            pass_diagonal(d - 2)
    for copy in small3:
        copy.wait_recv()

    def scored(r, best):
        scores = lax.dot_general(
            held[r], held[0], (((1,), (1,)), ((), ())), preferred_element_type=jnp.float32
        )
        key = column(keys[r])
        allowed = (key >= query_low) & (key < query_key)
        return jnp.maximum(
            best, jnp.max(jnp.where(allowed, scores, -1.0), axis=0, keepdims=True)
        )

    best = jnp.full((1, rows), -1.0, jnp.float32)
    if tree:
        pass_on(groups - 1)
        pass_diagonal(groups - 2)
        best = scored(0, best)
        for r in (2, 4):
            best = scored(r, best)
        pass_diagonal(groups - 1)
        for r in (1, 3, 5):
            for d in range(groups):
                arrive(r, d)
            best = scored(r, best)
        best = scored(6, best)
        for d in range(groups):
            for part in (0, 1):
                arrive(7, d, part)
        best = scored(7, best)
    else:
        best = scored(0, best)
        for r in range(1, members):
            for d in range(groups):
                arrive(r, d)
            best = scored(r, best)

    score2[...] = best
    home2 = [
        push(score2, back2.at[d], b2_send.at[d], b2_recv.at[d], (flip(z, d), m))
        for d in range(groups - 1, 0, -1)
    ]
    for copy in home2:
        copy.wait_recv()
    merged = best
    for d in range(1, groups):
        merged = jnp.where(lax.div(lane, share) == d, back2[d], merged)
    best = jnp.max(jnp.where(sub == slot2, column(merged), -2.0), axis=0, keepdims=True)
    score1[...] = best
    home1 = [
        push(score1, back1.at[r], b1_send.at[r], b1_recv.at[r], (z, flip(m, r)))
        for r in range(members - 1, 0, -1)
    ]
    for copy in home1:
        copy.wait_recv()
    merged = best
    for r in range(1, members):
        merged = jnp.where(lax.div(lane, deal) == r, back1[r], merged)
    out_ref[...] = jnp.max(jnp.where(sub == slot1, column(merged), -2.0), axis=0, keepdims=True)

    for copy in [
        *small,
        *copies1,
        *small2,
        *copies2.values(),
        *small3,
        *gathers.values(),
        *home2,
        *home1,
    ]:
        copy.wait_send()


def body(embeddings, cluster_ids, ranks):
    rows, features = embeddings.shape
    groups = lax.axis_size("group")
    members = lax.axis_size("member")
    scores = pl.pallas_call(
        functools.partial(kernel, groups, members),
        out_shape=jax.ShapeDtypeStruct((1, rows), jnp.float32),
        in_specs=[pl.BlockSpec(memory_space=pl.ANY)] * 3,
        out_specs=pl.BlockSpec(memory_space=pltpu.VMEM),
        scratch_shapes=[
            pltpu.VMEM((rows, features), jnp.bfloat16),
            pltpu.VMEM((1, rows), jnp.int32),
            pltpu.VMEM((1, rows), jnp.int32),
            pltpu.VMEM((rows, features), jnp.bfloat16),
            pltpu.VMEM((rows, features), jnp.bfloat16),
            pltpu.VMEM((rows, features), jnp.bfloat16),
            pltpu.VMEM((rows, features), jnp.bfloat16),
            pltpu.VMEM((members, rows, features), jnp.bfloat16),
            pltpu.VMEM((1, rows), jnp.float32),
            pltpu.VMEM((members, 1, rows), jnp.float32),
            pltpu.VMEM((1, rows), jnp.float32),
            pltpu.VMEM((groups, 1, rows), jnp.float32),
            pltpu.VMEM((members, 1, rows), jnp.float32),
            pltpu.VMEM((1, rows), jnp.float32),
            pltpu.VMEM((groups, 1, rows), jnp.float32),
            pltpu.VMEM((1, rows), jnp.float32),
            pltpu.VMEM((members, 1, rows), jnp.float32),
            pltpu.SemaphoreType.DMA((3,)),
            pltpu.SemaphoreType.DMA((members,)),
            pltpu.SemaphoreType.DMA((members,)),
            pltpu.SemaphoreType.DMA((groups,)),
            pltpu.SemaphoreType.DMA((groups,)),
            pltpu.SemaphoreType.DMA((members, groups, 2)),
            pltpu.SemaphoreType.DMA((members, groups, 2)),
            pltpu.SemaphoreType.DMA((members,)),
            pltpu.SemaphoreType.DMA((members,)),
            pltpu.SemaphoreType.DMA((groups,)),
            pltpu.SemaphoreType.DMA((groups,)),
            pltpu.SemaphoreType.DMA((members,)),
            pltpu.SemaphoreType.DMA((members,)),
            pltpu.SemaphoreType.DMA((groups,)),
            pltpu.SemaphoreType.DMA((groups,)),
            pltpu.SemaphoreType.DMA((members,)),
            pltpu.SemaphoreType.DMA((members,)),
        ],
        compiler_params=pltpu.CompilerParams(
            collective_id=0, has_side_effects=True, vmem_limit_bytes=48 * 1024 * 1024
        ),
    )(embeddings, cluster_ids.reshape(1, rows), ranks.reshape(1, rows))
    return scores.reshape(rows)


def solution(mesh):
    return jax.shard_map(
        body,
        mesh=mesh,
        in_specs=(P(("group", "member"), None), P(("group", "member")), P(("group", "member"))),
        out_specs=P(("group", "member")),
        check_vma=False,
    )
```

```python
import functools
import math

import jax
import jax.numpy as jnp
from jax import lax
from jax.experimental import pallas as pl
from jax.experimental.pallas import tpu as pltpu
from jax.sharding import PartitionSpec as P

HALVES = 2


def flip(index, mask):
    result = index
    bit = 1
    while bit <= mask:
        if mask & bit:
            result = result + bit - 2 * bit * lax.rem(lax.div(index, bit), 2)
        bit *= 2
    return result


def kernel(
    groups,
    members,
    emb_ref,
    ids_ref,
    ranks_ref,
    out_ref,
    emb,
    ids_row,
    ranks_row,
    packed,
    send1,
    recv1,
    send2,
    held,
    key1,
    keyin1,
    key2,
    keyin2,
    keys,
    score2,
    back2,
    score1,
    back1,
    local,
    s1_send,
    s1_recv,
    s2_send,
    s2_recv,
    ag_send,
    ag_recv,
    k1_send,
    k1_recv,
    k2_send,
    k2_recv,
    k3_send,
    k3_recv,
    b2_send,
    b2_recv,
    b1_send,
    b1_recv,
):
    rows, features = emb_ref.shape
    part = rows // HALVES
    deal = part // members
    share = part // groups
    z = lax.axis_index("group")
    m = lax.axis_index("member")

    loads = [
        pltpu.make_async_copy(src, dst, local.at[n])
        for n, (src, dst) in enumerate(
            ((ids_ref, ids_row), (ranks_ref, ranks_row), (emb_ref, emb))
        )
    ]
    for load in loads:
        load.start()
    barrier = pltpu.get_barrier_semaphore()
    for r in range(1, members):
        pl.semaphore_signal(
            barrier, inc=1, device_id=(z, flip(m, r)), device_id_type=pl.DeviceIdType.MESH
        )
    for d in range(1, groups):
        pl.semaphore_signal(
            barrier, inc=1, device_id=(flip(z, d), m), device_id_type=pl.DeviceIdType.MESH
        )

    def push(src, dst, send_sem, recv_sem, where):
        copy = pltpu.make_async_remote_copy(
            src_ref=src,
            dst_ref=dst,
            send_sem=send_sem,
            recv_sem=recv_sem,
            device_id=where,
            device_id_type=pl.DeviceIdType.MESH,
        )
        copy.start()
        return copy

    def column(row):
        return jnp.broadcast_to(row, (8, row.shape[1])).T[:, 0:1]

    sub = lax.broadcasted_iota(jnp.int32, (rows, rows), 0)
    lane = lax.broadcasted_iota(jnp.int32, (1, rows), 1)

    def order(bucket_row):
        key_row = (bucket_row * rows + lane).astype(jnp.float32)
        key_col = column(key_row)
        return jnp.sum((key_col < key_row).astype(jnp.float32), axis=0, keepdims=True).astype(
            jnp.int32
        )

    def permutation(slot):
        return (sub == slot).astype(jnp.float32).astype(jnp.bfloat16)

    def place_keys(ids, ranks, chosen):
        level = lax.broadcasted_iota(jnp.int32, (16, rows), 0)
        high = lax.div(ranks, 256)
        fields = jnp.where(
            level == 0, ids, jnp.where(level == 1, high, jnp.where(level == 2, ranks - high * 256, 0))
        )
        placed = lax.dot_general(
            fields.astype(jnp.float32).astype(jnp.bfloat16),
            chosen,
            (((1,), (1,)), ((), ())),
            preferred_element_type=jnp.float32,
        )
        return placed[0:1] * 65536.0 + placed[1:2] * 256.0 + placed[2:3]

    loads[0].wait()
    loads[1].wait()
    ids = ids_row[...]
    place = order(lax.rem(ids, groups))
    slot1 = (
        lax.rem(lax.div(place, members), HALVES) * part
        + jnp.bitwise_xor(lax.rem(place, members), m) * deal
        + lax.div(place, members * HALVES)
    )
    chosen1 = permutation(slot1)
    key1[...] = place_keys(ids, ranks_row[...], chosen1)
    loads[2].wait()
    widened = emb[...].astype(jnp.float32)
    square = jnp.mean(widened * widened, axis=-1, keepdims=True)
    packed[...] = (widened * lax.rsqrt(square + 1e-06) * (1.0 / math.sqrt(features))).astype(
        jnp.bfloat16
    )
    send1[...] = jnp.dot(chosen1, packed[...], preferred_element_type=jnp.float32).astype(
        jnp.bfloat16
    )
    pl.semaphore_wait(barrier, members + groups - 2)
    small = []
    for r in range(1, members):
        small.append(push(key1, keyin1.at[r], k1_send.at[r], k1_recv.at[r], (z, flip(m, r))))
    copies1 = {
        (h, r): push(
            send1.at[pl.ds(h * part + r * deal, deal)],
            recv1.at[pl.ds(h * part + r * deal, deal)],
            s1_send.at[h, r],
            s1_recv.at[h, r],
            (z, flip(m, r)),
        )
        for h in range(HALVES)
        for r in range(members - 1, 0, -1)
    }
    for h in range(HALVES):
        recv1[h * part : h * part + deal] = send1[h * part : h * part + deal]

    merged = key1[...]
    for r in range(1, members):
        small[r - 1].wait_recv()
        merged = jnp.where(lax.div(lax.rem(lane, part), deal) == r, keyin1[r], merged)
    merged = merged.astype(jnp.int32)
    ids = lax.div(merged, 65536)
    slot2 = order(lax.div(lane, part) * groups + jnp.bitwise_xor(lax.rem(ids, groups), z))
    chosen2 = permutation(slot2)
    key2[...] = place_keys(ids, merged - ids * 65536, chosen2)
    small2 = [
        push(key2, keyin2.at[d], k2_send.at[d], k2_recv.at[d], (flip(z, d), m))
        for d in range(1, groups)
    ]
    copies2 = {}

    def exchange(h):
        for r in range(1, members):
            copies1[(h, r)].wait_recv()
        first = h * part
        send2[first : first + part] = jnp.dot(
            chosen2[first : first + part, first : first + part],
            recv1[first : first + part],
            preferred_element_type=jnp.float32,
        ).astype(jnp.bfloat16)
        for d in range(1, groups):
            span = pl.ds(first + d * share, share)
            copies2[(h, d)] = push(
                send2.at[span],
                held.at[0, span],
                s2_send.at[h, d],
                s2_recv.at[h, d],
                (flip(z, d), m),
            )
        held[0, first : first + share] = send2[first : first + share]

    gathers = {}
    arrived = set()
    half = share // 2

    def forward(source, slot, chunk, side, hop):
        h, d = chunk
        start = h * part + d * share + (0 if side is None else side * half)
        span = pl.ds(start, share if side is None else half)
        index = (slot, h * groups + d, side or 0)
        gathers[(slot, chunk, side)] = push(
            held.at[source, span],
            held.at[slot, span],
            ag_send.at[index],
            ag_recv.at[index],
            (z, flip(m, hop)),
        )

    def arrive(slot, chunk, side=None):
        if (slot, chunk, side) not in arrived:
            gathers[(slot, chunk, side)].wait_recv()
            arrived.add((slot, chunk, side))

    tree = members == 8 and groups == 4

    def own_chunk(chunk):
        if chunk[1]:
            copies2[chunk].wait_recv()
        for r in (2, 4, 1) if tree else range(1, members):
            forward(0, r, chunk, None, r)

    def pass_on(chunk):
        arrive(2, chunk)
        forward(2, 6, chunk, 0, 4)
        forward(2, 3, chunk, None, 1)
        arrive(4, chunk)
        forward(4, 6, chunk, 1, 2)
        forward(4, 5, chunk, None, 1)

    def pass_diagonal(chunk):
        for side in (0, 1):
            arrive(6, chunk, side)
            forward(6, 7, chunk, side, 1)

    chunks = [(h, 0) for h in range(HALVES)]
    chunks += [(h, d) for h in range(HALVES) for d in range(1, groups)]
    for h in range(HALVES):
        exchange(h)
        own_chunk((h, 0))
    merged = key2[...]
    for d in range(1, groups):
        small2[d - 1].wait_recv()
        merged = jnp.where(lax.div(lax.rem(lane, part), share) == d, keyin2[d], merged)
    keys[0] = merged
    small3 = [
        push(keys.at[0], keys.at[r], k3_send.at[r], k3_recv.at[r], (z, flip(m, r)))
        for r in range(1, members)
    ]
    query_key = merged
    query_low = (lax.div(merged.astype(jnp.int32), 65536) * 65536).astype(jnp.float32)

    if tree:
        pass_on(chunks[0])
    for n in range(HALVES, len(chunks)):
        own_chunk(chunks[n])
        if tree:
            pass_on(chunks[n - 1])
            pass_diagonal(chunks[n - 2])
    for copy in small3:
        copy.wait_recv()

    def scored(r, h, best):
        first = h * part
        if r:
            for d in range(groups):
                for side in (0, 1) if tree and r >= 6 else (None,):
                    arrive(r, (h, d), side)
        scores = lax.dot_general(
            held[r, first : first + part],
            held[0],
            (((1,), (1,)), ((), ())),
            preferred_element_type=jnp.float32,
        )
        key = column(keys[r][:, first : first + part])
        allowed = (key >= query_low) & (key < query_key)
        return jnp.maximum(
            best, jnp.max(jnp.where(allowed, scores, -1.0), axis=0, keepdims=True)
        )

    best = jnp.full((1, rows), -1.0, jnp.float32)
    for h in range(HALVES):
        best = scored(0, h, best)
    if tree:
        pass_on(chunks[-1])
        pass_diagonal(chunks[-2])
        for r in (2, 4, 1, 3, 5):
            best = scored(r, 0, best)
        pass_diagonal(chunks[-1])
        for r, h in ((6, 0), (7, 0), (2, 1), (4, 1), (1, 1), (6, 1), (3, 1), (5, 1), (7, 1)):
            best = scored(r, h, best)
    else:
        for r in range(1, members):
            for h in range(HALVES):
                best = scored(r, h, best)

    score2[...] = best
    home2 = [
        push(score2, back2.at[d], b2_send.at[d], b2_recv.at[d], (flip(z, d), m))
        for d in range(groups - 1, 0, -1)
    ]
    for copy in home2:
        copy.wait_recv()
    merged = best
    for d in range(1, groups):
        merged = jnp.where(lax.div(lax.rem(lane, part), share) == d, back2[d], merged)
    best = jnp.max(jnp.where(sub == slot2, column(merged), -2.0), axis=0, keepdims=True)
    score1[...] = best
    home1 = [
        push(score1, back1.at[r], b1_send.at[r], b1_recv.at[r], (z, flip(m, r)))
        for r in range(members - 1, 0, -1)
    ]
    for copy in home1:
        copy.wait_recv()
    merged = best
    for r in range(1, members):
        merged = jnp.where(lax.div(lax.rem(lane, part), deal) == r, back1[r], merged)
    out_ref[...] = jnp.max(jnp.where(sub == slot1, column(merged), -2.0), axis=0, keepdims=True)

    for copy in [
        *small,
        *copies1.values(),
        *small2,
        *copies2.values(),
        *small3,
        *gathers.values(),
        *home2,
        *home1,
    ]:
        copy.wait_send()


def body(embeddings, cluster_ids, ranks):
    rows, features = embeddings.shape
    groups = lax.axis_size("group")
    members = lax.axis_size("member")
    scores = pl.pallas_call(
        functools.partial(kernel, groups, members),
        out_shape=jax.ShapeDtypeStruct((1, rows), jnp.float32),
        in_specs=[pl.BlockSpec(memory_space=pl.ANY)] * 3,
        out_specs=pl.BlockSpec(memory_space=pltpu.VMEM),
        scratch_shapes=[
            pltpu.VMEM((rows, features), jnp.bfloat16),
            pltpu.VMEM((1, rows), jnp.int32),
            pltpu.VMEM((1, rows), jnp.int32),
            pltpu.VMEM((rows, features), jnp.bfloat16),
            pltpu.VMEM((rows, features), jnp.bfloat16),
            pltpu.VMEM((rows, features), jnp.bfloat16),
            pltpu.VMEM((rows, features), jnp.bfloat16),
            pltpu.VMEM((members, rows, features), jnp.bfloat16),
            pltpu.VMEM((1, rows), jnp.float32),
            pltpu.VMEM((members, 1, rows), jnp.float32),
            pltpu.VMEM((1, rows), jnp.float32),
            pltpu.VMEM((groups, 1, rows), jnp.float32),
            pltpu.VMEM((members, 1, rows), jnp.float32),
            pltpu.VMEM((1, rows), jnp.float32),
            pltpu.VMEM((groups, 1, rows), jnp.float32),
            pltpu.VMEM((1, rows), jnp.float32),
            pltpu.VMEM((members, 1, rows), jnp.float32),
            pltpu.SemaphoreType.DMA((3,)),
            pltpu.SemaphoreType.DMA((HALVES, members)),
            pltpu.SemaphoreType.DMA((HALVES, members)),
            pltpu.SemaphoreType.DMA((HALVES, groups)),
            pltpu.SemaphoreType.DMA((HALVES, groups)),
            pltpu.SemaphoreType.DMA((members, HALVES * groups, 2)),
            pltpu.SemaphoreType.DMA((members, HALVES * groups, 2)),
            pltpu.SemaphoreType.DMA((members,)),
            pltpu.SemaphoreType.DMA((members,)),
            pltpu.SemaphoreType.DMA((groups,)),
            pltpu.SemaphoreType.DMA((groups,)),
            pltpu.SemaphoreType.DMA((members,)),
            pltpu.SemaphoreType.DMA((members,)),
            pltpu.SemaphoreType.DMA((groups,)),
            pltpu.SemaphoreType.DMA((groups,)),
            pltpu.SemaphoreType.DMA((members,)),
            pltpu.SemaphoreType.DMA((members,)),
        ],
        compiler_params=pltpu.CompilerParams(
            collective_id=0, has_side_effects=True, vmem_limit_bytes=48 * 1024 * 1024
        ),
    )(embeddings, cluster_ids.reshape(1, rows), ranks.reshape(1, rows))
    return scores.reshape(rows)


def solution(mesh):
    return jax.shard_map(
        body,
        mesh=mesh,
        in_specs=(P(("group", "member"), None), P(("group", "member")), P(("group", "member"))),
        out_specs=P(("group", "member")),
        check_vma=False,
    )
```

```python
import functools
import math

import jax
import jax.numpy as jnp
from jax import lax
from jax.experimental import pallas as pl
from jax.experimental.pallas import tpu as pltpu
from jax.sharding import PartitionSpec as P

HALVES = 2


def flip(index, mask):
    result = index
    bit = 1
    while bit <= mask:
        if mask & bit:
            result = result + bit - 2 * bit * lax.rem(lax.div(index, bit), 2)
        bit *= 2
    return result


def kernel(
    groups,
    members,
    emb_ref,
    ids_ref,
    ranks_ref,
    out_ref,
    emb,
    ids_row,
    ranks_row,
    packed,
    send1,
    recv1,
    send2,
    held,
    key1,
    keyin1,
    key2,
    keyin2,
    keys,
    score2,
    back2,
    score1,
    back1,
    local,
    s1_send,
    s1_recv,
    s2_send,
    s2_recv,
    ag_send,
    ag_recv,
    k1_send,
    k1_recv,
    k2_send,
    k2_recv,
    k3_send,
    k3_recv,
    b2_send,
    b2_recv,
    b1_send,
    b1_recv,
):
    rows, features = emb_ref.shape
    part = rows // HALVES
    deal = part // members
    share = part // groups
    z = lax.axis_index("group")
    m = lax.axis_index("member")

    loads = [
        pltpu.make_async_copy(src, dst, local.at[n])
        for n, (src, dst) in enumerate(
            ((ids_ref, ids_row), (ranks_ref, ranks_row), (emb_ref, emb))
        )
    ]
    for load in loads:
        load.start()
    barrier = pltpu.get_barrier_semaphore()
    for r in range(1, members):
        pl.semaphore_signal(
            barrier, inc=1, device_id=(z, flip(m, r)), device_id_type=pl.DeviceIdType.MESH
        )
    for d in range(1, groups):
        pl.semaphore_signal(
            barrier, inc=1, device_id=(flip(z, d), m), device_id_type=pl.DeviceIdType.MESH
        )

    def push(src, dst, send_sem, recv_sem, where):
        copy = pltpu.make_async_remote_copy(
            src_ref=src,
            dst_ref=dst,
            send_sem=send_sem,
            recv_sem=recv_sem,
            device_id=where,
            device_id_type=pl.DeviceIdType.MESH,
        )
        copy.start()
        return copy

    def column(row):
        return jnp.broadcast_to(row, (8, row.shape[1])).T[:, 0:1]

    sub = lax.broadcasted_iota(jnp.int32, (rows, rows), 0)
    lane = lax.broadcasted_iota(jnp.int32, (1, rows), 1)

    def order(bucket_row):
        key_row = (bucket_row * rows + lane).astype(jnp.float32)
        key_col = column(key_row)
        return jnp.sum((key_col < key_row).astype(jnp.float32), axis=0, keepdims=True).astype(
            jnp.int32
        )

    def permutation(slot):
        return (sub == slot).astype(jnp.float32).astype(jnp.bfloat16)

    def place_keys(ids, ranks, chosen):
        level = lax.broadcasted_iota(jnp.int32, (16, rows), 0)
        high = lax.div(ranks, 256)
        fields = jnp.where(
            level == 0, ids, jnp.where(level == 1, high, jnp.where(level == 2, ranks - high * 256, 0))
        )
        placed = lax.dot_general(
            fields.astype(jnp.float32).astype(jnp.bfloat16),
            chosen,
            (((1,), (1,)), ((), ())),
            preferred_element_type=jnp.float32,
        )
        return placed[0:1] * 65536.0 + placed[1:2] * 256.0 + placed[2:3]

    loads[0].wait()
    loads[1].wait()
    ids = ids_row[...]
    place = order(lax.rem(ids, groups))
    slot1 = (
        lax.rem(lax.div(place, members), HALVES) * part
        + jnp.bitwise_xor(lax.rem(place, members), m) * deal
        + lax.div(place, members * HALVES)
    )
    chosen1 = permutation(slot1)
    key1[...] = place_keys(ids, ranks_row[...], chosen1)
    loads[2].wait()
    widened = emb[...].astype(jnp.float32)
    square = jnp.mean(widened * widened, axis=-1, keepdims=True)
    packed[...] = (widened * lax.rsqrt(square + 1e-06) * (1.0 / math.sqrt(features))).astype(
        jnp.bfloat16
    )
    send1[...] = jnp.dot(chosen1, packed[...], preferred_element_type=jnp.float32).astype(
        jnp.bfloat16
    )
    pl.semaphore_wait(barrier, members + groups - 2)
    small = []
    for r in range(1, members):
        small.append(push(key1, keyin1.at[r], k1_send.at[r], k1_recv.at[r], (z, flip(m, r))))
    copies1 = {
        (h, r): push(
            send1.at[pl.ds(h * part + r * deal, deal)],
            recv1.at[pl.ds(h * part + r * deal, deal)],
            s1_send.at[h, r],
            s1_recv.at[h, r],
            (z, flip(m, r)),
        )
        for h in range(HALVES)
        for r in range(members - 1, 0, -1)
    }
    for h in range(HALVES):
        recv1[h * part : h * part + deal] = send1[h * part : h * part + deal]

    merged = key1[...]
    for r in range(1, members):
        small[r - 1].wait_recv()
        merged = jnp.where(lax.div(lax.rem(lane, part), deal) == r, keyin1[r], merged)
    merged = merged.astype(jnp.int32)
    ids = lax.div(merged, 65536)
    slot2 = order(lax.div(lane, part) * groups + jnp.bitwise_xor(lax.rem(ids, groups), z))
    chosen2 = permutation(slot2)
    key2[...] = place_keys(ids, merged - ids * 65536, chosen2)
    small2 = [
        push(key2, keyin2.at[d], k2_send.at[d], k2_recv.at[d], (flip(z, d), m))
        for d in range(1, groups)
    ]
    copies2 = {}

    def exchange(h):
        for r in range(1, members):
            copies1[(h, r)].wait_recv()
        first = h * part
        send2[first : first + part] = jnp.dot(
            chosen2[first : first + part, first : first + part],
            recv1[first : first + part],
            preferred_element_type=jnp.float32,
        ).astype(jnp.bfloat16)
        for d in range(1, groups):
            span = pl.ds(first + d * share, share)
            copies2[(h, d)] = push(
                send2.at[span],
                held.at[0, span],
                s2_send.at[h, d],
                s2_recv.at[h, d],
                (flip(z, d), m),
            )
        held[0, first : first + share] = send2[first : first + share]

    gathers = {}
    arrived = set()
    half = share // 2

    def forward(source, slot, chunk, side, hop):
        h, d = chunk
        start = h * part + d * share + (0 if side is None else side * half)
        span = pl.ds(start, share if side is None else half)
        index = (slot, h * groups + d, side or 0)
        gathers[(slot, chunk, side)] = push(
            held.at[source, span],
            held.at[slot, span],
            ag_send.at[index],
            ag_recv.at[index],
            (z, flip(m, hop)),
        )

    def arrive(slot, chunk, side=None):
        if (slot, chunk, side) not in arrived:
            gathers[(slot, chunk, side)].wait_recv()
            arrived.add((slot, chunk, side))

    tree = members == 8 and groups == 4

    def own_chunk(chunk):
        if chunk[1]:
            copies2[chunk].wait_recv()
        near = (2, 4, 1) if sum(chunk) % 2 == 0 else (4, 2, 1)
        for r in near if tree else range(1, members):
            forward(0, r, chunk, None, r)

    def pass_on(chunk):
        arrive(2, chunk)
        forward(2, 6, chunk, 0, 4)
        forward(2, 3, chunk, None, 1)
        arrive(4, chunk)
        forward(4, 6, chunk, 1, 2)
        forward(4, 5, chunk, None, 1)

    def pass_diagonal(chunk):
        for side in (0, 1):
            arrive(6, chunk, side)
            forward(6, 7, chunk, side, 1)

    chunks = [(h, 0) for h in range(HALVES)]
    chunks += [(h, d) for h in range(HALVES) for d in range(1, groups)]
    for h in range(HALVES):
        exchange(h)
        own_chunk((h, 0))
    merged = key2[...]
    for d in range(1, groups):
        small2[d - 1].wait_recv()
        merged = jnp.where(lax.div(lax.rem(lane, part), share) == d, keyin2[d], merged)
    keys[0] = merged
    small3 = [
        push(keys.at[0], keys.at[r], k3_send.at[r], k3_recv.at[r], (z, flip(m, r)))
        for r in range(1, members)
    ]
    query_key = merged
    query_low = (lax.div(merged.astype(jnp.int32), 65536) * 65536).astype(jnp.float32)

    if tree:
        pass_on(chunks[0])
    for n in range(HALVES, len(chunks)):
        own_chunk(chunks[n])
        if tree:
            pass_on(chunks[n - 1])
            pass_diagonal(chunks[n - 2])
    for copy in small3:
        copy.wait_recv()

    def scored(r, h, best):
        first = h * part
        if r:
            for d in range(groups):
                for side in (0, 1) if tree and r >= 6 else (None,):
                    arrive(r, (h, d), side)
        scores = lax.dot_general(
            held[r, first : first + part],
            held[0],
            (((1,), (1,)), ((), ())),
            preferred_element_type=jnp.float32,
        )
        key = column(keys[r][:, first : first + part])
        allowed = (key >= query_low) & (key < query_key)
        return jnp.maximum(
            best, jnp.max(jnp.where(allowed, scores, -1.0), axis=0, keepdims=True)
        )

    best = jnp.full((1, rows), -1.0, jnp.float32)
    for h in range(HALVES):
        best = scored(0, h, best)
    if tree:
        pass_on(chunks[-1])
        pass_diagonal(chunks[-2])
        for r in (2, 4, 1, 3, 5):
            best = scored(r, 0, best)
        pass_diagonal(chunks[-1])
        for r, h in ((6, 0), (7, 0), (2, 1), (4, 1), (1, 1), (6, 1), (3, 1), (5, 1), (7, 1)):
            best = scored(r, h, best)
    else:
        for r in range(1, members):
            for h in range(HALVES):
                best = scored(r, h, best)

    score2[...] = best
    home2 = [
        push(score2, back2.at[d], b2_send.at[d], b2_recv.at[d], (flip(z, d), m))
        for d in range(groups - 1, 0, -1)
    ]
    for copy in home2:
        copy.wait_recv()
    merged = best
    for d in range(1, groups):
        merged = jnp.where(lax.div(lax.rem(lane, part), share) == d, back2[d], merged)
    best = jnp.max(jnp.where(sub == slot2, column(merged), -2.0), axis=0, keepdims=True)
    score1[...] = best
    home1 = [
        push(score1, back1.at[r], b1_send.at[r], b1_recv.at[r], (z, flip(m, r)))
        for r in range(members - 1, 0, -1)
    ]
    for copy in home1:
        copy.wait_recv()
    merged = best
    for r in range(1, members):
        merged = jnp.where(lax.div(lax.rem(lane, part), deal) == r, back1[r], merged)
    out_ref[...] = jnp.max(jnp.where(sub == slot1, column(merged), -2.0), axis=0, keepdims=True)

    for copy in [
        *small,
        *copies1.values(),
        *small2,
        *copies2.values(),
        *small3,
        *gathers.values(),
        *home2,
        *home1,
    ]:
        copy.wait_send()


def body(embeddings, cluster_ids, ranks):
    rows, features = embeddings.shape
    groups = lax.axis_size("group")
    members = lax.axis_size("member")
    scores = pl.pallas_call(
        functools.partial(kernel, groups, members),
        out_shape=jax.ShapeDtypeStruct((1, rows), jnp.float32),
        in_specs=[pl.BlockSpec(memory_space=pl.ANY)] * 3,
        out_specs=pl.BlockSpec(memory_space=pltpu.VMEM),
        scratch_shapes=[
            pltpu.VMEM((rows, features), jnp.bfloat16),
            pltpu.VMEM((1, rows), jnp.int32),
            pltpu.VMEM((1, rows), jnp.int32),
            pltpu.VMEM((rows, features), jnp.bfloat16),
            pltpu.VMEM((rows, features), jnp.bfloat16),
            pltpu.VMEM((rows, features), jnp.bfloat16),
            pltpu.VMEM((rows, features), jnp.bfloat16),
            pltpu.VMEM((members, rows, features), jnp.bfloat16),
            pltpu.VMEM((1, rows), jnp.float32),
            pltpu.VMEM((members, 1, rows), jnp.float32),
            pltpu.VMEM((1, rows), jnp.float32),
            pltpu.VMEM((groups, 1, rows), jnp.float32),
            pltpu.VMEM((members, 1, rows), jnp.float32),
            pltpu.VMEM((1, rows), jnp.float32),
            pltpu.VMEM((groups, 1, rows), jnp.float32),
            pltpu.VMEM((1, rows), jnp.float32),
            pltpu.VMEM((members, 1, rows), jnp.float32),
            pltpu.SemaphoreType.DMA((3,)),
            pltpu.SemaphoreType.DMA((HALVES, members)),
            pltpu.SemaphoreType.DMA((HALVES, members)),
            pltpu.SemaphoreType.DMA((HALVES, groups)),
            pltpu.SemaphoreType.DMA((HALVES, groups)),
            pltpu.SemaphoreType.DMA((members, HALVES * groups, 2)),
            pltpu.SemaphoreType.DMA((members, HALVES * groups, 2)),
            pltpu.SemaphoreType.DMA((members,)),
            pltpu.SemaphoreType.DMA((members,)),
            pltpu.SemaphoreType.DMA((groups,)),
            pltpu.SemaphoreType.DMA((groups,)),
            pltpu.SemaphoreType.DMA((members,)),
            pltpu.SemaphoreType.DMA((members,)),
            pltpu.SemaphoreType.DMA((groups,)),
            pltpu.SemaphoreType.DMA((groups,)),
            pltpu.SemaphoreType.DMA((members,)),
            pltpu.SemaphoreType.DMA((members,)),
        ],
        compiler_params=pltpu.CompilerParams(
            collective_id=0, has_side_effects=True, vmem_limit_bytes=48 * 1024 * 1024
        ),
    )(embeddings, cluster_ids.reshape(1, rows), ranks.reshape(1, rows))
    return scores.reshape(rows)


def solution(mesh):
    return jax.shard_map(
        body,
        mesh=mesh,
        in_specs=(P(("group", "member"), None), P(("group", "member")), P(("group", "member"))),
        out_specs=P(("group", "member")),
        check_vma=False,
    )
```
